32 devices in a mesh: fsdp: 4 (over y, x), dp: 8 (over z, core).
Axes of the slice: x: 2, y: 2, z: 4, core: 2. Of those that a mesh axis runs over, the one named last changes fastest.
Arguments:
- tokens: bfloat16 [4, 2112, 3200], P('fsdp', 'dp'), may hold values from -6 to 6
- norm_gain: float32 [3200], replicated, may hold values from 0.5 to 1.5
- qkv_weight: bfloat16 [3200, 3072], P('fsdp', 'dp'), may hold values from -4 to 4
- qk_gain: float32 [2, 1024], P(None, 'dp'), may hold values from 1 to 8
- out_weight: bfloat16 [1024, 3200], P('dp', 'fsdp'), may hold values from -0.1875 to 0.1875
- layer_scale: float32 [3200], replicated, may hold values from 0.2 to 1
- tile_counts: int32 [4, 2], replicated, may hold values from 0 to 2, as said below
- owners: int32 [4, 2], replicated, may hold values from 0 to 3, as said below
Outputs:
- vision_tokens: bfloat16 [16, 256, 12800], P('fsdp', None, 'dp')
The draws below stay inside these ranges and needn't reach their ends.
Inputs may be any that keep to these rules, and one draw needn't show every extreme that they name: `tile_counts`: column 0 is 1 to 2, column 1 is 0 to 2 minus column 0. All owners together get at most 4 live tiles each, and one owner gets exactly 4.
All inputs are finite; a program needn't handle non-finite values.
Results may differ from the reference program's by a relative error of at most 0.006.
The reference program's roundings to bfloat16 on the way count: a program that leaves them out, or rounds other values in their place, can miss the bound.
Values may be sent and summed in bfloat16 or wider, within the bound.
A program may use at most 192 MiB of HBM per device.

```python
import math
import jax
import jax.numpy as jnp
from jax import lax

D = 3200
HEAD_DIM = 128
GRID = 32
SLOTS = 2
HEADS = 8
ROWS = 4
TILE = 1025
ROW_LEN = 2112
CAP = 4


def routing_pair(key):
    base_key = jax.random.fold_in(key, 7)
    first_key, second_key, order_key = jax.random.split(base_key, 3)
    row_index = jnp.arange(ROWS, dtype=jnp.int32)
    first_count = jax.random.randint(first_key, (ROWS,), 1, SLOTS + 1, dtype=jnp.int32)
    first_count = jnp.where(row_index < 2, SLOTS, first_count)
    second_count = jax.random.randint(second_key, (ROWS,), 0, SLOTS - first_count + 1, dtype=jnp.int32)
    counts = jnp.stack([first_count, second_count], axis=1).astype(jnp.int32)
    ordering = jax.random.permutation(order_key, ROWS).astype(jnp.int32)
    owner_first = ordering[row_index // 2]
    owner_second = ordering[ROWS // 2 + row_index // 2]
    return (counts, jnp.stack([owner_first, owner_second], axis=1).astype(jnp.int32))


def draw_tile_counts(key, part):
    return routing_pair(key)[0]


def draw_owners(key, part):
    return routing_pair(key)[1]


def draw_qkv_weight(key, part):
    standard = jnp.clip(jax.random.normal(key, (D, HEADS * 3 * HEAD_DIM), jnp.float32), -4.0, 4.0)
    column = jnp.arange(HEADS * 3 * HEAD_DIM, dtype=jnp.int32)
    head_index = (column // (3 * HEAD_DIM)).astype(jnp.float32)
    part_index = column // HEAD_DIM % 3
    position_ratio = head_index / max(HEADS - 1, 1)
    factor = 0.6 * jnp.power(3.0, position_ratio)
    factor = jnp.where(part_index < 2, factor, 1.0)
    return (standard * factor[None, :] * D ** (-0.5)).astype(jnp.bfloat16)


def draw_qk_gain(key, part):
    uniform_draw = jax.random.uniform(key, (2, HEADS * HEAD_DIM), jnp.float32)
    lower_log = jnp.log(1.0)
    upper_log = jnp.log(3.0)
    return jnp.exp(lower_log + (upper_log - lower_log) * uniform_draw)


def block_scale(key, dims, cuts, least, top_value):
    def one(dim, blocks):
        steps = jax.random.uniform(jax.random.fold_in(jax.random.fold_in(key, 6), dim), (blocks,), jnp.float32, least / len(cuts), top_value / len(cuts))
        return jnp.repeat(jnp.exp(steps), dims[dim] // blocks).reshape((-1,) + (1,) * (len(dims) - dim - 1))

    level = one(*cuts[0])
    for cut in cuts[1:]:
        level = level * one(*cut)
    return level


def normal_values(key, extent, width, most, pieces=(), kind=jnp.bfloat16):
    drawn = jax.random.normal(key, extent, jnp.float32) * width
    if len(pieces) > 0:
        drawn = block_scale(key, extent, pieces, -0.22, 0.18) * drawn
    return jnp.clip(drawn, min=-most, max=most).astype(kind)


def setup_inputs(seed: int = 0) -> dict:
    keys = jax.random.split(jax.random.key(seed), 9)
    return {
        "tokens": normal_values(keys[0], (ROWS, ROW_LEN, D), 1.0, 6.0, ((0, 4), (1, 8))),
        "norm_gain": jnp.clip(1.0 + 0.1 * jax.random.normal(keys[1], (D,), jnp.float32), 0.5, 1.5),
        "qkv_weight": draw_qkv_weight(jax.random.fold_in(keys[8], 71), 0),
        "qk_gain": draw_qk_gain(jax.random.fold_in(keys[8], 71), 0),
        "out_weight": normal_values(keys[4], (HEADS * HEAD_DIM, D), (HEADS * HEAD_DIM) ** -0.5, 0.1875, ((0, 8), (1, 4))),
        "layer_scale": jnp.clip(jnp.exp(jax.random.uniform(keys[5], (D,), jnp.float32, math.log(0.2), math.log(1.0))), 0.2, 1.0),
        "tile_counts": draw_tile_counts(jax.random.fold_in(keys[8], 71), 0),
        "owners": draw_owners(jax.random.fold_in(keys[8], 71), 0),
    }


EPSILON = 1e-06

def merge_tiles(values):
    halves = GRID // 2
    columns = values.shape[1]
    tile_list = []
    for tile_slot in range(SLOTS):
        patches = values[tile_slot * TILE + 1:(tile_slot + 1) * TILE]
        square = patches.reshape(halves, 2, halves, 2, columns).transpose(0, 2, 4, 1, 3)
        tile_list.append(square.reshape(halves * halves, columns * 4))
    return jnp.stack(tile_list)

def tile_owners(tile_counts, owners):
    slot_index = jnp.arange(SLOTS, dtype=jnp.int32)[None, :]
    first_count = tile_counts[:, 0:1]
    holder = jnp.where(slot_index < first_count, owners[:, 0:1], owners[:, 1:2])
    living = slot_index < first_count + tile_counts[:, 1:2]
    return (holder, living)

def place_tiles(received, holder, living, target):
    owned_flag = jnp.logical_and(living, holder == target).reshape(-1).astype(jnp.int32)
    before = jnp.cumsum(owned_flag) - owned_flag
    chosen = jnp.logical_and(before[None, :] == jnp.arange(CAP, dtype=jnp.int32)[:, None], owned_flag[None, :] == 1)
    flattened = received.reshape(received.shape[0] * received.shape[1], -1)
    placed = jnp.dot(chosen.astype(jnp.bfloat16), flattened, preferred_element_type=jnp.float32)
    return placed.astype(jnp.bfloat16).reshape(CAP, received.shape[2], received.shape[3])

def attend_row(tokens_row, live_count, norm_gain, qkv_weight, qk_gain, out_weight, layer_scale):
    length = tokens_row.shape[0]
    model_width = tokens_row.shape[1]
    head_count = qk_gain.shape[1] // HEAD_DIM
    window = head_count * HEAD_DIM
    values = tokens_row.astype(jnp.float32)
    normed = (values * lax.rsqrt(lax.optimization_barrier(jnp.mean(values * values, axis=-1, keepdims=True)) + EPSILON) * norm_gain).astype(jnp.bfloat16)
    projected = jnp.dot(normed, qkv_weight, preferred_element_type=jnp.float32).reshape(length, head_count, 3, HEAD_DIM)
    queries = projected[:, :, 0]
    keys_part = projected[:, :, 1]
    values_part = projected[:, :, 2].astype(jnp.bfloat16)
    query_gain = qk_gain[0].reshape(head_count, HEAD_DIM)
    key_gain = qk_gain[1].reshape(head_count, HEAD_DIM)
    queries = (queries * lax.rsqrt(lax.optimization_barrier(jnp.sum(queries * queries, axis=(1, 2), keepdims=True)) / window + EPSILON) * query_gain).astype(jnp.bfloat16)
    keys_part = (keys_part * lax.rsqrt(lax.optimization_barrier(jnp.sum(keys_part * keys_part, axis=(1, 2), keepdims=True)) / window + EPSILON) * key_gain).astype(jnp.bfloat16)
    position = jnp.arange(length, dtype=jnp.int32)
    segment = jnp.minimum(position // TILE, live_count)
    same_tile = segment[:, None] == segment[None, :]
    factor = HEAD_DIM ** (-0.5)

    def head_step(running, inputs):
        query_head, key_head, value_head, weight_head = inputs
        scores = jnp.dot(query_head, key_head.T, preferred_element_type=jnp.float32) * factor
        scores = jnp.where(same_tile, scores, -1e+30)
        highest = lax.optimization_barrier(jnp.max(scores, axis=-1, keepdims=True))
        exponent = jnp.exp(scores - highest)
        weights = (exponent / lax.optimization_barrier(jnp.sum(exponent, axis=-1, keepdims=True))).astype(jnp.bfloat16)
        attended = jnp.dot(weights, value_head, preferred_element_type=jnp.float32).astype(jnp.bfloat16)
        head_term = jnp.dot(attended, weight_head, preferred_element_type=jnp.float32).astype(jnp.bfloat16)
        head_term = lax.optimization_barrier(head_term)
        return (running + head_term.astype(jnp.float32), None)
    inputs = (queries.transpose(1, 0, 2), keys_part.transpose(1, 0, 2), values_part.transpose(1, 0, 2), out_weight.reshape(head_count, HEAD_DIM, model_width))
    attention, unused = lax.scan(head_step, jnp.zeros((length, model_width), jnp.float32), inputs)
    updated = (values + layer_scale * attention).astype(jnp.bfloat16)
    return merge_tiles(updated)

def reference(tokens, norm_gain, qkv_weight, qk_gain, out_weight, layer_scale, tile_counts, owners):
    merged_rows = []
    for row_index in range(ROWS):
        live_count = (tile_counts[row_index, 0] + tile_counts[row_index, 1]).astype(jnp.int32)
        merged_rows.append(attend_row(tokens[row_index], live_count, norm_gain, qkv_weight, qk_gain, out_weight, layer_scale))
    received = jnp.stack(merged_rows)
    holder, living = tile_owners(tile_counts, owners)
    placed_list = [place_tiles(received, holder, living, target) for target in range(ROWS)]
    return jnp.concatenate(placed_list, axis=0)
```

```python
import jax
import jax.numpy as jnp
from jax import lax
from jax.experimental import pallas as pl
from jax.experimental.pallas import tpu as pltpu
from jax.sharding import PartitionSpec as P

HEAD_DIM = 128
GRID = 32
SLOTS = 2
TILE = 1025
CAP = 4
HALF = GRID // 2
CELLS = HALF * HALF
EPSILON = 1e-06


def patch_order(values):
    columns = values.shape[-1]
    square = values.reshape(HALF, 2, HALF, 2, columns).transpose(1, 3, 0, 2, 4)
    return square.reshape(4 * CELLS, columns)


def project_kernel(att_ref, weight_ref, token_ref, scale_ref, out_ref):
    places, rows, _ = token_ref.shape
    width = token_ref.shape[2]
    groups = att_ref.shape[0]
    total = jnp.zeros((places * rows, width), jnp.float32)
    for group in range(groups):
        for part in range(2):
            block = att_ref[group, :, :, part * HEAD_DIM : (part + 1) * HEAD_DIM]
            term = jnp.dot(
                block.reshape(places * rows, HEAD_DIM),
                weight_ref[part * groups + group],
                preferred_element_type=jnp.float32,
            )
            total = total + term.astype(jnp.bfloat16).astype(jnp.float32)
    tokens = token_ref[...].reshape(places * rows, width).astype(jnp.float32)
    updated = (tokens + scale_ref[...] * total).astype(jnp.bfloat16)
    for start in range(0, width, 128):
        size = min(128, width - start)
        feature = lax.broadcasted_iota(jnp.int32, (size, 4 * size), 0)
        lane = lax.broadcasted_iota(jnp.int32, (size, 4 * size), 1)
        merged = jnp.zeros((rows, 4 * size), jnp.float32)
        for place in range(4):
            spread = jnp.where(lane == 4 * feature + place, 1.0, 0.0).astype(jnp.bfloat16)
            merged = merged + jnp.dot(
                updated[place * rows : (place + 1) * rows, start : start + size],
                spread,
                preferred_element_type=jnp.float32,
            )
        out_ref[:, 4 * start : 4 * (start + size)] = merged.astype(jnp.bfloat16)


def project_merge(attended, weight, tokens, scale):
    groups = attended.shape[0]
    heads, width = weight.shape[1], weight.shape[3]
    rows = 64
    return pl.pallas_call(
        project_kernel,
        grid=(2, CELLS // rows),
        in_specs=[
            pl.BlockSpec((groups, 4, rows, 2 * HEAD_DIM), lambda s, m: (0, 0, m, 0)),
            pl.BlockSpec((None, heads, HEAD_DIM, width), lambda s, m: (s, 0, 0, 0)),
            pl.BlockSpec((None, 4, rows, width), lambda s, m: (s, 0, m, 0)),
            pl.BlockSpec((None, 1, width), lambda s, m: (s, 0, 0)),
        ],
        out_specs=pl.BlockSpec((None, rows, 4 * width), lambda s, m: (s, m, 0)),
        out_shape=jax.ShapeDtypeStruct((2, CELLS, 4 * width), jnp.bfloat16),
        compiler_params=pltpu.CompilerParams(vmem_limit_bytes=40 * 2**20),
        name="project_merge",
    )(attended, weight, tokens, scale)


def place_kernel(row_ref, which_ref, valid_ref, first_ref, second_ref, out_ref):
    slot = pl.program_id(0)
    valid = valid_ref[slot] == 1
    first = jnp.logical_and(valid, which_ref[slot] == 0)
    second = jnp.logical_and(valid, which_ref[slot] == 1)

    @pl.when(first)
    def _():
        out_ref[...] = first_ref[...]

    @pl.when(second)
    def _():
        out_ref[...] = second_ref[...]

    @pl.when(jnp.logical_not(valid))
    def _():
        out_ref[...] = jnp.zeros_like(out_ref)


def place_tiles(first, second, row, which, valid):
    _, cells, columns = first.shape
    block = (None, cells, columns)
    return pl.pallas_call(
        place_kernel,
        grid_spec=pltpu.PrefetchScalarGridSpec(
            num_scalar_prefetch=3,
            grid=(CAP,),
            in_specs=[
                pl.BlockSpec(block, lambda k, r, w, v: (r[k], 0, 0)),
                pl.BlockSpec(block, lambda k, r, w, v: (r[k], 0, 0)),
            ],
            out_specs=pl.BlockSpec(block, lambda k, r, w, v: (k, 0, 0)),
        ),
        out_shape=jax.ShapeDtypeStruct((CAP, cells, columns), jnp.bfloat16),
        name="place_tiles",
    )(row, which, valid, first, second)


def slot_choice(tile_counts, owners, target):
    slot_index = jnp.arange(SLOTS, dtype=jnp.int32)[None, :]
    first_count = tile_counts[:, 0:1]
    holder = jnp.where(slot_index < first_count, owners[:, 0:1], owners[:, 1:2])
    living = slot_index < first_count + tile_counts[:, 1:2]
    owned = jnp.logical_and(living, holder == target).reshape(-1).astype(jnp.int32)
    order = jnp.arange(owned.shape[0], dtype=jnp.int32)
    before = jnp.sum(jnp.where(order[None, :] < order[:, None], owned[None, :], 0), axis=1)
    chosen = jnp.logical_and(
        before[None, :] == jnp.arange(CAP, dtype=jnp.int32)[:, None], owned[None, :] == 1
    )
    tile = jnp.sum(jnp.where(chosen, order[None, :], 0), axis=1)
    return tile // SLOTS, tile % SLOTS, jnp.any(chosen, axis=1).astype(jnp.int32)


def body(tokens, norm_gain, qkv_weight, qk_gain, out_weight, layer_scale, tile_counts, owners):
    own_rows = tokens[0]
    width_all = own_rows.shape[1]
    devices = lax.axis_size("dp")
    group = devices // 2
    position = lax.axis_index("dp")
    lower = position < group
    inner = position % group
    pairs = [list(range(group)), list(range(group, devices))]
    across = [(j, (j + group) % devices) for j in range(devices)]
    upward = [(j, j + group) for j in range(group)]

    gathered = lax.all_gather(own_rows, "dp", axis=0, tiled=True, axis_index_groups=pairs)
    other_block = lax.ppermute(qkv_weight, "dp", across)
    other_gain = lax.ppermute(qk_gain, "dp", across)
    own_weight = lax.all_gather(qkv_weight, "fsdp", axis=0, tiled=True)
    other_weight = lax.all_gather(other_block, "fsdp", axis=0, tiled=True)
    length = gathered.shape[0]
    spill = length - TILE

    def tile_of(values, spilled):
        moved = jnp.concatenate([spilled, values[: TILE - spill]], axis=0)
        return jnp.where(lower, values[:TILE], moved)

    values = gathered.astype(jnp.float32)
    normed = (
        values * lax.rsqrt(jnp.mean(values * values, axis=-1, keepdims=True) + EPSILON) * norm_gain
    ).astype(jnp.bfloat16)
    projected = [
        jnp.dot(normed, weight, preferred_element_type=jnp.float32)
        for weight in (own_weight, other_weight)
    ]
    queries = [part[:, :HEAD_DIM] for part in projected]
    keys = [part[:, HEAD_DIM : 2 * HEAD_DIM] for part in projected]
    vals = [part[:, 2 * HEAD_DIM :].astype(jnp.bfloat16) for part in projected]
    sums = jnp.stack(
        [
            sum(jnp.sum(q * q, axis=-1) for q in queries),
            sum(jnp.sum(k * k, axis=-1) for k in keys),
        ]
    )
    step = 1
    while step < group:
        swap = [(j, j ^ step) for j in range(devices)]
        sums = sums + lax.ppermute(sums, "dp", swap)
        step *= 2
    window = devices * HEAD_DIM
    factors = lax.rsqrt(sums / window + EPSILON)
    gains = (qk_gain, other_gain)
    queries = [
        (q * factors[0][:, None] * g[0]).astype(jnp.bfloat16) for q, g in zip(queries, gains)
    ]
    keys = [(k * factors[1][:, None] * g[1]).astype(jnp.bfloat16) for k, g in zip(keys, gains)]
    parts = [queries[0], queries[1], keys[0], keys[1], vals[0], vals[1]]
    swapped = [queries[1], queries[0], keys[1], keys[0], vals[1], vals[0]]
    spilled = lax.ppermute(
        jnp.concatenate([part[TILE:] for part in swapped], axis=1), "dp", upward
    )
    tiles = [
        tile_of(part, spilled[:, n * HEAD_DIM : (n + 1) * HEAD_DIM])
        for n, part in enumerate(parts)
    ]
    query = jnp.stack([patch_order(tiles[0][1:]), patch_order(tiles[1][1:])])
    key = jnp.stack(tiles[2:4])
    value = jnp.stack(tiles[4:6])
    factor = HEAD_DIM ** (-0.5)
    scores = jnp.einsum("sqc,skc->sqk", query, key, preferred_element_type=jnp.float32) * factor
    highest = jnp.max(scores, axis=-1, keepdims=True)
    exponent = jnp.exp(scores - highest)
    weights = (exponent / jnp.sum(exponent, axis=-1, keepdims=True)).astype(jnp.bfloat16)
    attended = jnp.einsum(
        "sqk,skc->sqc", weights, value, preferred_element_type=jnp.float32
    ).astype(jnp.bfloat16)
    both = jnp.where(
        lower,
        jnp.concatenate([attended[0], attended[1]], axis=1),
        jnp.concatenate([attended[1], attended[0]], axis=1),
    )
    heads_here = lax.all_gather(both, "dp", axis=0, axis_index_groups=pairs)
    heads_here = heads_here.reshape(group, 4, CELLS, 2 * HEAD_DIM)

    portion = width_all // group
    half_width = portion // 2
    weight_rows = lax.all_gather(out_weight, "dp", axis=0, tiled=True)
    if lax.axis_size("fsdp") == group:
        weight_full = lax.all_gather(weight_rows, "fsdp", axis=0)
        weight_here = lax.dynamic_index_in_dim(weight_full, inner, 0, keepdims=False)
    else:
        weight_full = lax.all_gather(weight_rows, "fsdp", axis=1, tiled=True)
        weight_here = lax.dynamic_slice_in_dim(weight_full, inner * portion, portion, 1)
    weight_here = weight_here.reshape(devices, HEAD_DIM, 2, half_width).transpose(2, 0, 1, 3)
    token_part = lax.dynamic_slice_in_dim(gathered, inner * portion, portion, 1)
    token_spill = lax.ppermute(token_part[TILE:], "dp", upward)
    token_tile = patch_order(tile_of(token_part, token_spill)[1:])
    token_tile = token_tile.reshape(4, CELLS, 2, half_width).transpose(2, 0, 1, 3)
    scale_here = lax.dynamic_slice_in_dim(layer_scale, inner * portion, portion, 0)
    merged = project_merge(heads_here, weight_here, token_tile, scale_here.reshape(2, 1, half_width))

    part_index = jnp.where(lower, 0, 1)
    first_out = lax.dynamic_index_in_dim(merged, part_index, 0, keepdims=False)
    second_out = lax.dynamic_index_in_dim(merged, 1 - part_index, 0, keepdims=False)
    straight = [(j, 2 * j) for j in range(group)] + [(group + j, 2 * j + 1) for j in range(group)]
    crossed = [(j, 2 * j + 1) for j in range(group)] + [(group + j, 2 * j) for j in range(group)]
    first_all = lax.all_gather(lax.ppermute(first_out, "dp", straight), "fsdp", axis=0)
    second_all = lax.all_gather(lax.ppermute(second_out, "dp", crossed), "fsdp", axis=0)
    row, slot, valid = slot_choice(tile_counts, owners, lax.axis_index("fsdp"))
    which = slot ^ (position % 2)
    return place_tiles(first_all, second_all, row, which, valid)


def solution(mesh):
    placed = (
        P("fsdp", "dp", None),
        P(),
        P("fsdp", "dp"),
        P(None, "dp"),
        P("dp", "fsdp"),
        P(),
        P(),
        P(),
    )
    return jax.shard_map(
        body, mesh=mesh, in_specs=placed, out_specs=P("fsdp", None, "dp"), check_vma=False
    )
```

```python
import functools

import jax
import jax.numpy as jnp
from jax import lax
from jax.experimental import pallas as pl
from jax.experimental.pallas import tpu as pltpu
from jax.sharding import PartitionSpec as P

HEAD_DIM = 128
GRID = 32
SLOTS = 2
TILE = 1025
CAP = 4
HALF = GRID // 2
CELLS = HALF * HALF
EPSILON = 1e-06


def patch_order(values):
    columns = values.shape[-1]
    square = values.reshape(HALF, 2, HALF, 2, columns).transpose(1, 3, 0, 2, 4)
    return square.reshape(4 * CELLS, columns)


def project_kernel(att_ref, weight_ref, token_ref, scale_ref, out_ref):
    places, rows, _ = token_ref.shape
    width = token_ref.shape[2]
    groups = att_ref.shape[0]
    total = jnp.zeros((places * rows, width), jnp.float32)
    for group in range(groups):
        for part in range(2):
            block = att_ref[group, :, :, part * HEAD_DIM : (part + 1) * HEAD_DIM]
            term = jnp.dot(
                block.reshape(places * rows, HEAD_DIM),
                weight_ref[part * groups + group],
                preferred_element_type=jnp.float32,
            )
            total = total + term.astype(jnp.bfloat16).astype(jnp.float32)
    tokens = token_ref[...].reshape(places * rows, width).astype(jnp.float32)
    updated = (tokens + scale_ref[...] * total).astype(jnp.bfloat16)
    for start in range(0, width, 128):
        size = min(128, width - start)
        feature = lax.broadcasted_iota(jnp.int32, (size, 4 * size), 0)
        lane = lax.broadcasted_iota(jnp.int32, (size, 4 * size), 1)
        merged = jnp.zeros((rows, 4 * size), jnp.float32)
        for place in range(4):
            spread = jnp.where(lane == 4 * feature + place, 1.0, 0.0).astype(jnp.bfloat16)
            merged = merged + jnp.dot(
                updated[place * rows : (place + 1) * rows, start : start + size],
                spread,
                preferred_element_type=jnp.float32,
            )
        out_ref[:, 4 * start : 4 * (start + size)] = merged.astype(jnp.bfloat16)


def project_merge(attended, weight, tokens, scale):
    groups = attended.shape[0]
    heads, width = weight.shape[1], weight.shape[3]
    rows = 64
    return pl.pallas_call(
        project_kernel,
        grid=(2, CELLS // rows),
        in_specs=[
            pl.BlockSpec((groups, 4, rows, 2 * HEAD_DIM), lambda s, m: (0, 0, m, 0)),
            pl.BlockSpec((None, heads, HEAD_DIM, width), lambda s, m: (s, 0, 0, 0)),
            pl.BlockSpec((None, 4, rows, width), lambda s, m: (s, 0, m, 0)),
            pl.BlockSpec((None, 1, width), lambda s, m: (s, 0, 0)),
        ],
        out_specs=pl.BlockSpec((None, rows, 4 * width), lambda s, m: (s, m, 0)),
        out_shape=jax.ShapeDtypeStruct((2, CELLS, 4 * width), jnp.bfloat16),
        compiler_params=pltpu.CompilerParams(vmem_limit_bytes=40 * 2**20),
        name="project_merge",
    )(attended, weight, tokens, scale)


MESH = pl.DeviceIdType.MESH


def gather_kernel(
    fsdp_size, dp_size, rows_ref, qkv_ref, proj_ref, tokens_out, qkv_out, proj_out,
    local_sem, row_send, row_recv, qkv_send, qkv_recv, proj_send, proj_recv,
):
    mine, position = lax.axis_index("fsdp"), lax.axis_index("dp")
    group = dp_size // 2
    half = position // group
    inner = position - half * group
    base = half * group
    partner = lax.rem(position + group, dp_size)
    sibling = base + (inner + 1 - 2 * lax.rem(inner, 2))
    chips = group // 2
    near = [base + lax.rem(inner + 2 * r, group) for r in range(1, chips)]
    across = [lax.rem(mine + r, fsdp_size) for r in range(1, fsdp_size)]

    barrier = pltpu.get_barrier_semaphore()
    fixed = [(mine, p) for p in near + [sibling, partner]] + [(f, position) for f in across]
    for target in fixed:
        pl.semaphore_signal(barrier, inc=1, device_id=target, device_id_type=MESH)
    for source in range(dp_size):

        @pl.when(jnp.logical_or(mine != inner, position != source))
        def _():
            pl.semaphore_signal(barrier, inc=1, device_id=(inner, source), device_id_type=MESH)

    pl.semaphore_wait(barrier, len(fixed) + 2 * fsdp_size - jnp.where(mine == inner, 1, 0))

    def send(src, dst, send_sem, recv_sem, target):
        copy = pltpu.make_async_remote_copy(
            src_ref=src, dst_ref=dst, send_sem=send_sem, recv_sem=recv_sem,
            device_id=target, device_id_type=MESH,
        )
        copy.start()
        return copy

    def arrived(ref, sem):
        pltpu.make_async_copy(ref, ref, sem).wait()

    sent = []
    sent.append(send(qkv_ref, qkv_out.at[1, mine], qkv_send.at[0], qkv_recv.at[1, mine], (mine, partner)))
    for n, peer in enumerate(near):
        sent.append(send(rows_ref, tokens_out.at[inner], row_send.at[n], row_recv.at[inner], (mine, peer)))
    sent.append(
        send(rows_ref, tokens_out.at[inner], row_send.at[chips], row_recv.at[inner], (mine, sibling))
    )
    for n, peer in enumerate(across):
        sent.append(
            send(qkv_ref, qkv_out.at[0, mine], qkv_send.at[1 + n], qkv_recv.at[0, mine], (peer, position))
        )
    own_rows = pltpu.make_async_copy(rows_ref, tokens_out.at[inner], local_sem.at[0])
    own_qkv = pltpu.make_async_copy(qkv_ref, qkv_out.at[0, mine], local_sem.at[1])
    own_rows.start()
    own_qkv.start()

    def proj_copy(row, side):
        slot = row * 2 + side
        return pltpu.make_async_remote_copy(
            src_ref=proj_ref, dst_ref=proj_out.at[position], send_sem=proj_send.at[slot],
            recv_sem=proj_recv.at[position], device_id=(row, side * group + mine), device_id_type=MESH,
        )

    own_proj = pltpu.make_async_copy(proj_ref, proj_out.at[position], local_sem.at[2])

    def each_proj(action):
        for row in range(fsdp_size):
            for side in range(2):

                @pl.when(jnp.logical_or(row != mine, side * group + mine != position))
                def _():
                    action(proj_copy(row, side))

    each_proj(lambda copy: copy.start())

    @pl.when(mine == inner)
    def _():
        own_proj.start()

    arrived(qkv_out.at[1, mine], qkv_recv.at[1, mine])
    for n, peer in enumerate(across):
        sent.append(
            send(qkv_out.at[1, mine], qkv_out.at[1, mine], qkv_send.at[fsdp_size + n],
                 qkv_recv.at[1, mine], (peer, position))
        )
    for n in range(1, chips):
        block = lax.rem(inner + 2 * (chips - n), group)
        arrived(tokens_out.at[block], row_recv.at[block])
        sent.append(
            send(tokens_out.at[block], tokens_out.at[block], row_send.at[chips + n],
                 row_recv.at[block], (mine, sibling))
        )
    other = inner + 1 - 2 * lax.rem(inner, 2)
    for n in range(chips):
        block = lax.rem(other + 2 * n, group)
        arrived(tokens_out.at[block], row_recv.at[block])
    for peer in across:
        for kind in range(2):
            arrived(qkv_out.at[kind, peer], qkv_recv.at[kind, peer])
    for source in range(dp_size):

        @pl.when(jnp.logical_or(mine != inner, position != source))
        def _():
            arrived(proj_out.at[source], proj_recv.at[source])

    for copy in sent:
        copy.wait_send()
    each_proj(lambda copy: copy.wait_send())
    own_rows.wait()
    own_qkv.wait()

    @pl.when(mine == inner)
    def _():
        own_proj.wait()


def gather_inputs(rows, qkv, proj):
    fsdp_size, dp_size = lax.axis_size("fsdp"), lax.axis_size("dp")
    group = dp_size // 2
    anywhere = pl.BlockSpec(memory_space=pl.ANY)
    dma = pltpu.SemaphoreType.DMA
    return pl.pallas_call(
        functools.partial(gather_kernel, fsdp_size, dp_size),
        in_specs=[anywhere] * 3,
        out_specs=[anywhere] * 3,
        out_shape=[
            jax.ShapeDtypeStruct((group,) + rows.shape, rows.dtype),
            jax.ShapeDtypeStruct((2, fsdp_size) + qkv.shape, qkv.dtype),
            jax.ShapeDtypeStruct((dp_size,) + proj.shape, proj.dtype),
        ],
        scratch_shapes=[
            dma((3,)),
            dma((group,)),
            dma((group,)),
            dma((2 * fsdp_size - 1,)),
            dma((2, fsdp_size)),
            dma((2 * fsdp_size,)),
            dma((dp_size,)),
        ],
        compiler_params=pltpu.CompilerParams(collective_id=0, has_side_effects=True),
        name="gather_inputs",
    )(rows, qkv, proj)


PIECES = 4


def deliver_kernel(
    fsdp_size, dp_size, merged_ref, out_ref, local_sem, first_send, first_recv, next_send, next_recv
):
    mine, position = lax.axis_index("fsdp"), lax.axis_index("dp")
    group = dp_size // 2
    half = position // group
    inner = position - half * group
    across = [lax.rem(mine + r, fsdp_size) for r in range(1, fsdp_size)]
    size = merged_ref.shape[1] // PIECES
    barrier = pltpu.get_barrier_semaphore()
    for peer in across:
        pl.semaphore_signal(barrier, inc=1, device_id=(peer, position), device_id_type=MESH)
    origin = position // 2
    for side in range(2):

        @pl.when(side * group + origin != position)
        def _():
            pl.semaphore_signal(
                barrier, inc=1, device_id=(mine, side * group + origin), device_id_type=MESH
            )

    pl.semaphore_wait(barrier, len(across) + 2 - jnp.where(origin == inner, 1, 0))

    def first_copy(part, piece):
        place = pl.ds(piece * size, size)
        return pltpu.make_async_remote_copy(
            src_ref=merged_ref.at[part, place], dst_ref=out_ref.at[mine, half, place],
            send_sem=first_send.at[part, piece], recv_sem=first_recv.at[half, piece],
            device_id=(mine, 2 * inner + part), device_id_type=MESH,
        )

    def own_copy(part, piece):
        place = pl.ds(piece * size, size)
        return pltpu.make_async_copy(
            merged_ref.at[part, place], out_ref.at[mine, half, place], local_sem.at[piece]
        )

    for piece in range(PIECES):
        for part in range(2):

            @pl.when(2 * inner + part != position)
            def _():
                first_copy(part, piece).start()

            @pl.when(2 * inner + part == position)
            def _():
                own_copy(part, piece).start()

    sent = []
    for piece in range(PIECES):
        place = pl.ds(piece * size, size)
        for side in range(2):
            ref = out_ref.at[mine, side, place]
            here = side * group + origin == position

            @pl.when(jnp.logical_not(here))
            def _():
                pltpu.make_async_copy(ref, ref, first_recv.at[side, piece]).wait()

            @pl.when(here)
            def _():
                pltpu.make_async_copy(ref, ref, local_sem.at[piece]).wait()

            for n, peer in enumerate(across):
                copy = pltpu.make_async_remote_copy(
                    src_ref=ref, dst_ref=ref, send_sem=next_send.at[n, side, piece],
                    recv_sem=next_recv.at[mine, side, piece],
                    device_id=(peer, position), device_id_type=MESH,
                )
                copy.start()
                sent.append(copy)
    for piece in range(PIECES):
        place = pl.ds(piece * size, size)
        for side in range(2):
            for peer in across:
                ref = out_ref.at[peer, side, place]
                pltpu.make_async_copy(ref, ref, next_recv.at[peer, side, piece]).wait()
    for copy in sent:
        copy.wait_send()
    for piece in range(PIECES):
        for part in range(2):

            @pl.when(2 * inner + part != position)
            def _():
                first_copy(part, piece).wait_send()


def deliver(merged):
    fsdp_size, dp_size = lax.axis_size("fsdp"), lax.axis_size("dp")
    dma = pltpu.SemaphoreType.DMA
    return pl.pallas_call(
        functools.partial(deliver_kernel, fsdp_size, dp_size),
        in_specs=[pl.BlockSpec(memory_space=pl.ANY)],
        out_specs=pl.BlockSpec(memory_space=pl.ANY),
        out_shape=jax.ShapeDtypeStruct((fsdp_size,) + merged.shape, merged.dtype),
        scratch_shapes=[
            dma((PIECES,)),
            dma((2, PIECES)),
            dma((2, PIECES)),
            dma((fsdp_size - 1, 2, PIECES)),
            dma((fsdp_size, 2, PIECES)),
        ],
        compiler_params=pltpu.CompilerParams(collective_id=1, has_side_effects=True),
        name="deliver",
    )(merged)


def place_kernel(tile_ref, valid_ref, all_ref, out_ref):
    valid = valid_ref[pl.program_id(0)] == 1

    @pl.when(valid)
    def _():
        out_ref[...] = all_ref[...]

    @pl.when(jnp.logical_not(valid))
    def _():
        out_ref[...] = jnp.zeros_like(out_ref)


def place_tiles(tiles, tile, valid):
    _, cells, columns = tiles.shape
    block = (None, cells, columns)
    return pl.pallas_call(
        place_kernel,
        grid_spec=pltpu.PrefetchScalarGridSpec(
            num_scalar_prefetch=2,
            grid=(CAP,),
            in_specs=[pl.BlockSpec(block, lambda k, t, v: (t[k], 0, 0))],
            out_specs=pl.BlockSpec(block, lambda k, t, v: (k, 0, 0)),
        ),
        out_shape=jax.ShapeDtypeStruct((CAP, cells, columns), jnp.bfloat16),
        name="place_tiles",
    )(tile, valid, tiles)


def slot_choice(tile_counts, owners, target):
    slot_index = jnp.arange(SLOTS, dtype=jnp.int32)[None, :]
    first_count = tile_counts[:, 0:1]
    holder = jnp.where(slot_index < first_count, owners[:, 0:1], owners[:, 1:2])
    living = slot_index < first_count + tile_counts[:, 1:2]
    owned = jnp.logical_and(living, holder == target).reshape(-1).astype(jnp.int32)
    order = jnp.arange(owned.shape[0], dtype=jnp.int32)
    before = jnp.sum(jnp.where(order[None, :] < order[:, None], owned[None, :], 0), axis=1)
    chosen = jnp.logical_and(
        before[None, :] == jnp.arange(CAP, dtype=jnp.int32)[:, None], owned[None, :] == 1
    )
    tile = jnp.sum(jnp.where(chosen, order[None, :], 0), axis=1)
    return tile, jnp.any(chosen, axis=1).astype(jnp.int32)


def body(tokens, norm_gain, qkv_weight, qk_gain, out_weight, layer_scale, tile_counts, owners):
    own_rows = tokens[0]
    width_all = own_rows.shape[1]
    devices = lax.axis_size("dp")
    group = devices // 2
    position = lax.axis_index("dp")
    lower = position < group
    inner = position % group
    pairs = [list(range(group)), list(range(group, devices))]
    across = [(j, (j + group) % devices) for j in range(devices)]
    upward = [(j, j + group) for j in range(group)]

    if lax.axis_size("fsdp") != group:
        raise ValueError("mesh axes")
    gathered, weights_qkv, weight_here = gather_inputs(own_rows, qkv_weight, out_weight)
    gathered = gathered.reshape(-1, width_all)
    weights_qkv = weights_qkv.reshape(2, width_all, -1)
    own_weight, other_weight = weights_qkv[0], weights_qkv[1]
    other_gain = lax.ppermute(qk_gain, "dp", across)
    length = gathered.shape[0]
    spill = length - TILE

    def tile_of(values, spilled):
        moved = jnp.concatenate([spilled, values[: TILE - spill]], axis=0)
        return jnp.where(lower, values[:TILE], moved)

    values = gathered.astype(jnp.float32)
    normed = (
        values * lax.rsqrt(jnp.mean(values * values, axis=-1, keepdims=True) + EPSILON) * norm_gain
    ).astype(jnp.bfloat16)
    projected = [
        jnp.dot(normed, weight, preferred_element_type=jnp.float32)
        for weight in (own_weight, other_weight)
    ]
    queries = [part[:, :HEAD_DIM] for part in projected]
    keys = [part[:, HEAD_DIM : 2 * HEAD_DIM] for part in projected]
    vals = [part[:, 2 * HEAD_DIM :].astype(jnp.bfloat16) for part in projected]
    sums = jnp.stack(
        [
            sum(jnp.sum(q * q, axis=-1) for q in queries),
            sum(jnp.sum(k * k, axis=-1) for k in keys),
        ]
    )
    step = 1
    while step < group:
        swap = [(j, j ^ step) for j in range(devices)]
        sums = sums + lax.ppermute(sums, "dp", swap)
        step *= 2
    window = devices * HEAD_DIM
    factors = lax.rsqrt(sums / window + EPSILON)
    gains = (qk_gain, other_gain)
    queries = [
        (q * factors[0][:, None] * g[0]).astype(jnp.bfloat16) for q, g in zip(queries, gains)
    ]
    keys = [(k * factors[1][:, None] * g[1]).astype(jnp.bfloat16) for k, g in zip(keys, gains)]
    parts = [queries[0], queries[1], keys[0], keys[1], vals[0], vals[1]]
    swapped = [queries[1], queries[0], keys[1], keys[0], vals[1], vals[0]]
    spilled = lax.ppermute(
        jnp.concatenate([part[TILE:] for part in swapped], axis=1), "dp", upward
    )
    tiles = [
        tile_of(part, spilled[:, n * HEAD_DIM : (n + 1) * HEAD_DIM])
        for n, part in enumerate(parts)
    ]
    query = jnp.stack([patch_order(tiles[0][1:]), patch_order(tiles[1][1:])])
    key = jnp.stack(tiles[2:4])
    value = jnp.stack(tiles[4:6])
    factor = HEAD_DIM ** (-0.5)
    scores = jnp.einsum("sqc,skc->sqk", query, key, preferred_element_type=jnp.float32) * factor
    highest = jnp.max(scores, axis=-1, keepdims=True)
    exponent = jnp.exp(scores - highest)
    weights = (exponent / jnp.sum(exponent, axis=-1, keepdims=True)).astype(jnp.bfloat16)
    attended = jnp.einsum(
        "sqk,skc->sqc", weights, value, preferred_element_type=jnp.float32
    ).astype(jnp.bfloat16)
    both = jnp.where(
        lower,
        jnp.concatenate([attended[0], attended[1]], axis=1),
        jnp.concatenate([attended[1], attended[0]], axis=1),
    )
    heads_here = lax.all_gather(both, "dp", axis=0, axis_index_groups=pairs)
    heads_here = heads_here.reshape(group, 4, CELLS, 2 * HEAD_DIM)

    portion = width_all // group
    half_width = portion // 2
    weight_here = weight_here.reshape(devices, HEAD_DIM, 2, half_width).transpose(2, 0, 1, 3)
    token_part = lax.dynamic_slice_in_dim(gathered, inner * portion, portion, 1)
    token_spill = lax.ppermute(token_part[TILE:], "dp", upward)
    token_tile = patch_order(tile_of(token_part, token_spill)[1:])
    token_tile = token_tile.reshape(4, CELLS, 2, half_width).transpose(2, 0, 1, 3)
    scale_here = lax.dynamic_slice_in_dim(layer_scale, inner * portion, portion, 0)
    merged = project_merge(heads_here, weight_here, token_tile, scale_here.reshape(2, 1, half_width))

    delivered = deliver(merged)
    tile, valid = slot_choice(tile_counts, owners, lax.axis_index("fsdp"))
    return place_tiles(delivered.reshape((-1,) + delivered.shape[2:]), tile, valid)


def solution(mesh):
    placed = (
        P("fsdp", "dp", None),
        P(),
        P("fsdp", "dp"),
        P(None, "dp"),
        P("dp", "fsdp"),
        P(),
        P(),
        P(),
    )
    return jax.shard_map(
        body, mesh=mesh, in_specs=placed, out_specs=P("fsdp", None, "dp"), check_vma=False
    )
```
